128 devices in a mesh: section: 16 (over y_hi, x, core), dp: 8 (over z, y_lo).
Axes of the slice: x: 4, y: 4 (y_hi: 2, y_lo: 2; y = y_hi * 2 + y_lo), z: 4, core: 2. Of those that a mesh axis runs over, the one named last changes fastest.
Arguments:
- cotangent: bfloat16 [2, 128, 4096], P(None, None, 'dp'), may hold values from -3 to 3
- inputs: bfloat16 [16, 2, 128, 4096], P('section', None, None, 'dp'), may hold values from -6 to 6
- inv_rms: float32 [16, 2, 128], P('section'), may hold values from 0.1 to 0.4
- gain: float32 [16, 4096], P('section'), may hold values from 0.1 to 1.9
- weight: bfloat16 [16, 4096, 4096], P('section', None, 'dp'), may hold values from -0.09375 to 0.09375
Outputs:
- grad_in: bfloat16 [16, 2, 128, 4096], P('section', None, None, 'dp')
- weight_grad: float32 [16, 4096, 4096], P('section', None, 'dp')
- gain_grad: float32 [16, 4096], P('section', 'dp')
- row_dot: float32 [16, 2, 128], P('section')
The draws below stay inside these ranges and needn't reach their ends.
All inputs are finite; a program needn't handle non-finite values.
Results may differ from the reference program's by a relative error of at most 0.035.
Values may be sent and summed in bfloat16 or wider, within the bound.
A program may use at most 64 MiB of HBM per device.

```python
import math
import jax
import jax.numpy as jnp
from jax import lax

MODEL_WIDTH = 4096
MB_ROWS = 128
MICRO = 2
LAYERS = 16
N_DP = 8


def block_scale(stream_key, shape, pieces, smallest, largest):
    loudness, own = 1.0, jax.random.fold_in(stream_key, 6)
    for axis_at, blocks in pieces:
        heights = jnp.exp(jax.random.uniform(jax.random.fold_in(own, axis_at), (blocks,), jnp.float32, smallest / len(pieces), largest / len(pieces)))
        loudness = loudness * jnp.repeat(heights, shape[axis_at] // blocks).reshape([-1 if axis == axis_at else 1 for axis in range(len(shape))])
    return loudness


def bell_draw(own_key, shape, scale, limit, shards=(), kind=jnp.bfloat16):
    entries = jax.random.normal(own_key, shape, jnp.float32) * scale
    if len(shards) > 0:
        entries = block_scale(own_key, shape, shards, -0.22, 0.18) * entries
    return jnp.clip(entries, min=-limit, max=limit).astype(kind)


def setup_inputs(seed: int = 0) -> dict:
    arg_keys = jax.random.split(jax.random.key(seed), 6)
    cotangent = bell_draw(arg_keys[0], (MICRO, MB_ROWS, MODEL_WIDTH), 0.5, 3.0, ((2, 8),))
    inputs = bell_draw(arg_keys[1], (LAYERS, MICRO, MB_ROWS, MODEL_WIDTH), 1.0, 6.0, ((0, 16), (3, 8)))
    inv_rms = jnp.clip(jnp.exp(math.log(0.4) - 1.3862944 * jax.random.uniform(arg_keys[2], (LAYERS, MICRO, MB_ROWS), jnp.float32) ** block_scale(arg_keys[2], (LAYERS, MICRO, MB_ROWS), ((0, 16),), -0.2, 0.2)), 0.1, 0.4)
    gain = jnp.clip(1.0 + 0.18 * jax.random.normal(arg_keys[3], (LAYERS, MODEL_WIDTH), jnp.float32), 0.1, 1.9)
    weight = bell_draw(arg_keys[4], (LAYERS, MODEL_WIDTH, MODEL_WIDTH), MODEL_WIDTH ** -0.5, 0.09375, ((0, 16), (2, 8)))
    return {"cotangent": cotangent, "inputs": inputs, "inv_rms": inv_rms, "gain": gain, "weight": weight}


def reference(cotangent, inputs, inv_rms, gain, weight):
    per = MODEL_WIDTH // N_DP
    root_width = float(MODEL_WIDTH) ** 0.5
    token_scale = float(MICRO * MB_ROWS) ** -0.5

    def layer(carry_state, slices):
        input_rows, scale_factor, g, w = slices
        normalized_input = input_rows.astype(jnp.float32) * scale_factor[..., None]
        grouped = carry_state.astype(jnp.float32).reshape(MICRO, MB_ROWS, N_DP, per)
        w_groups = w.astype(jnp.float32).reshape(MODEL_WIDTH, N_DP, per)
        partial_sums = jnp.einsum("mrkj,ikj->kmri", grouped, w_groups)
        rounded = lax.optimization_barrier(partial_sums.astype(jnp.bfloat16))
        down_weight = jnp.sum(rounded.astype(jnp.float32), axis=0)
        gain_float = g.astype(jnp.float32)
        normed_gradient = down_weight * gain_float
        row_statistic = jnp.sum(normed_gradient * normalized_input, axis=-1) / MODEL_WIDTH
        row_output = row_statistic * root_width / scale_factor
        result_output = (carry_state.astype(jnp.float32) + scale_factor[..., None] * (normed_gradient - normalized_input * row_statistic[..., None])).astype(jnp.bfloat16)
        normed_input = (normalized_input * gain_float).astype(jnp.bfloat16)
        w_grad = jnp.dot(normed_input.reshape(-1, MODEL_WIDTH).T, carry_state.reshape(-1, MODEL_WIDTH), preferred_element_type=jnp.float32) * token_scale
        gain_gradient = jnp.sum(down_weight * normalized_input, axis=(0, 1)) * token_scale
        return result_output, (result_output, w_grad, gain_gradient, row_output)

    _, outputs = lax.scan(layer, cotangent, (inputs, inv_rms, gain, weight))
    return outputs[0], outputs[1], outputs[2], outputs[3]
```

```python
import functools

import jax
import jax.numpy as jnp
from jax import lax
from jax.experimental import pallas as pl
from jax.experimental.pallas import tpu as pltpu
from jax.sharding import PartitionSpec as P

MESH = pl.DeviceIdType.MESH
F32 = jnp.float32
BF16 = jnp.bfloat16
CHUNK = 16
GROUP = 64
FAR_FIRST = (5, 4, 3, 7, 2, 6, 1)
LAG = 3


def wide(block, times):
    return jnp.concatenate([block] * times, axis=1)


def chain_kernel(
    sections, n_dp, rows, cols,
    cot_ref, x_ref, r_ref, gain_ref, w_hbm,
    carry, gout, ggrad, rdot, normed_hbm,
    w, wt, xg, normed, u, xprev, rb, sb, rq, qbuf, g1, g1r, stat, statr,
    w_sem, xg_send, xg_recv, xp_send, xp_recv, rq_recv, q_send, back_send, back_recv,
    g1_send, g1_recv, st_send, st_recv, n_sem,
):
    s, d = lax.axis_index("section"), lax.axis_index("dp")
    last = sections - 1
    chunks, groups = rows // CHUNK, rows // GROUP
    width = n_dp * cols
    nxt = jnp.minimum(s + 1, last)
    prev = jnp.maximum(s - 1, 0)
    lanes = rb.shape[1]

    def peer(i):
        return (d + i) % n_dp

    def w_copy(k):
        part = pl.ds(pl.multiple_of(k * cols, cols), cols)
        return pltpu.make_async_copy(w_hbm.at[part, :], w.at[part, :], w_sem.at[k])

    @pl.loop(0, n_dp)
    def _(k):
        w_copy(k).start()

    barrier = pltpu.get_barrier_semaphore()

    @pl.loop(1, n_dp)
    def _(i):
        pl.semaphore_signal(barrier, inc=1, device_id=(s, peer(i)), device_id_type=MESH)

    @pl.when(s > 0)
    def _():
        @pl.loop(0, n_dp)
        def _(i):
            pl.semaphore_signal(barrier, inc=1, device_id=(prev, i), device_id_type=MESH)

    @pl.when(s < last)
    def _():
        @pl.loop(0, n_dp)
        def _(i):
            pl.semaphore_signal(barrier, inc=1, device_id=(nxt, i), device_id_type=MESH)

    for m in range(rows // lanes):
        rb[pl.ds(m * lanes, lanes), :] = jnp.broadcast_to(r_ref[pl.ds(m, 1), :], (lanes, lanes)).T
    g1[...] = jnp.zeros_like(g1)

    @pl.when(s == last)
    def _():
        g1r[...] = jnp.zeros_like(g1r)

    inner = jnp.logical_and(s > 0, s < last)
    pl.semaphore_wait(barrier, jnp.where(inner, 3 * n_dp - 1, 2 * n_dp - 1))

    def group_rows(g):
        return pl.ds(pl.multiple_of(g * GROUP, GROUP), GROUP)

    @pl.loop(0, groups)
    def _(g):
        part = group_rows(g)
        pltpu.make_async_copy(x_ref.at[part, :], xg.at[d, part, :], xg_recv.at[g]).start()

        @pl.loop(1, n_dp)
        def _(i):
            pltpu.make_async_remote_copy(
                x_ref.at[part, :], xg.at[d, part, :], xg_send, xg_recv.at[g],
                device_id=(s, peer(i)), device_id_type=MESH,
            ).start()

    @pl.when(s < last)
    def _():
        pltpu.make_async_remote_copy(
            x_ref, xprev, xp_send, xp_recv, device_id=(nxt, d), device_id_type=MESH
        ).start()

    @pl.loop(0, n_dp)
    def _(k):
        w_copy(k).wait()
        part = pl.ds(pl.multiple_of(k * cols, cols), cols)
        wt[:, part] = w[part, :].T

    def project(g):
        part = group_rows(g)
        pltpu.make_async_copy(xg.at[:, part, :], xg.at[:, part, :], xg_recv.at[g]).wait()
        scale = wide(rb[part, :], cols // lanes)

        @pl.loop(0, n_dp)
        def _(k):
            block = pl.ds(pl.multiple_of(k * cols, cols), cols)
            normed[part, block] = (
                xg[k, part, :].astype(F32) * scale * gain_ref[:, block]
            ).astype(BF16)

        pltpu.make_async_copy(normed.at[part, :], normed_hbm.at[part, :], n_sem.at[g]).start()
        u[part, :] = jnp.dot(normed[part, :], w[...], preferred_element_type=F32)

    early = jnp.where(s < 6, 1, groups)

    @pl.loop(0, early)
    def _(g):
        project(g)

    def chunk_rows(i):
        return pl.ds(pl.multiple_of(i * CHUNK, CHUNK), CHUNK)

    def total(slot):
        pltpu.make_async_copy(rq.at[slot], rq.at[slot], rq_recv.at[slot]).wait()
        added = rq[slot, 0].astype(F32)
        for k in range(1, n_dp):
            added += rq[slot, k].astype(F32)
        return added, (rq[slot, n_dp].astype(F32) + added).astype(BF16)

    def add_gain(where, x_rows, added):
        term = x_rows.astype(F32) * added
        for b in range(CHUNK // 8):
            where[...] += term[b * 8 : (b + 1) * 8, :]

    def finish(i):
        part = chunk_rows(i)
        added, result = total(chunks + i)
        gout[part, :] = result
        add_gain(g1r, x_ref[part, :], added)

    @pl.when(s > 0)
    def _():
        pltpu.make_async_copy(xprev, xprev, xp_recv).wait()

    @pl.loop(0, chunks)
    def _(i):
        part = chunk_rows(i)

        @pl.when(s == 0)
        def _():
            carry[part, :] = cot_ref[part, :]

        @pl.when(s > 0)
        def _():
            added, result = total(i)
            carry[part, :] = result
            pltpu.make_async_remote_copy(
                carry.at[part, :], gout.at[part, :], back_send, back_recv,
                device_id=(prev, d), device_id_type=MESH,
            ).start()
            add_gain(g1, xprev[part, :], added)

        slot = jnp.where(s == last, chunks + i, i)

        @pl.when(s < last)
        def _():
            pltpu.make_async_remote_copy(
                carry.at[part, :], rq.at[slot, n_dp], q_send, rq_recv.at[slot],
                device_id=(nxt, d), device_id_type=MESH,
            ).start()

        @pl.when(s == last)
        def _():
            pltpu.make_async_copy(carry.at[part, :], rq.at[slot, n_dp], rq_recv.at[slot]).start()

        mine = carry[part, :]
        scale = rb[part, :]
        dots = mine.astype(F32) * u[part, :]
        row = jnp.sum(dots, axis=1, keepdims=True) * (1.0 / width)
        row = jnp.broadcast_to(row, (CHUNK, lanes))
        sb[part, :] = row
        shift = wide(row * scale * scale, cols // lanes)
        scale = wide(scale, cols // lanes)

        def sums(f):
            block = pl.ds(pl.multiple_of(f * cols, cols), cols)
            product = jnp.dot(mine, wt[:, block], preferred_element_type=F32)
            qbuf[i, f] = (
                product * scale * gain_ref[:, block] - xg[f, part, :].astype(F32) * shift
            ).astype(BF16)

        for off in FAR_FIRST:
            f = d + off - 2 * sum(((d // b) % 2) * b for b in (1, 2, 4) if off & b)
            sums(f)
            pltpu.make_async_remote_copy(
                qbuf.at[i, f], rq.at[slot, d], q_send, rq_recv.at[slot],
                device_id=(nxt, f), device_id_type=MESH,
            ).start()
        sums(d)

        @pl.when(s < last)
        def _():
            pltpu.make_async_remote_copy(
                qbuf.at[i, d], rq.at[slot, d], q_send, rq_recv.at[slot],
                device_id=(nxt, d), device_id_type=MESH,
            ).start()

        @pl.when(s == last)
        def _():
            pltpu.make_async_copy(qbuf.at[i, d], rq.at[slot, d], rq_recv.at[slot]).start()

        per = GROUP // CHUNK

        @pl.when(jnp.logical_and(early == 1, jnp.logical_and(i % per == per // 2, i // per + 1 < groups)))
        def _():
            project(i // per + 1)

        @pl.when(jnp.logical_and(s == last, i >= LAG))
        def _():
            finish(i - LAG)

    stat[...] = jnp.zeros_like(stat)
    for m in range(rows // lanes):
        turned = sb[pl.ds(m * lanes, lanes), :].T
        stat[pl.ds(m, 1), :] = turned[0:1, :]

    pltpu.make_async_copy(stat, statr.at[d], st_recv).start()

    @pl.loop(1, n_dp)
    def _(i):
        pltpu.make_async_remote_copy(
            stat, statr.at[d], st_send, st_recv, device_id=(s, peer(i)), device_id_type=MESH
        ).start()

    @pl.when(s > 0)
    def _():
        pltpu.make_async_remote_copy(
            g1, g1r, g1_send, g1_recv, device_id=(prev, d), device_id_type=MESH
        ).start()
        pltpu.make_async_copy(g1, g1, g1_send).wait()

    @pl.when(s == last)
    def _():
        @pl.loop(chunks - LAG, chunks)
        def _(i):
            finish(i)

    pltpu.make_async_copy(statr, statr, st_recv).wait()
    rows_stat = statr[0]
    for k in range(1, n_dp):
        rows_stat += statr[k]
    halves = rows // lanes
    rdot[...] = rows_stat[:halves, :] * (float(width) ** 0.5) / r_ref[...]

    own = pl.ds(pl.multiple_of(d * cols, cols), cols)
    second = jnp.zeros((8, cols), F32)
    for m in range(halves):
        part = pl.ds(m * lanes, lanes)
        column = jnp.broadcast_to(rows_stat[m : m + 1, :], (lanes, lanes)).T
        factor = column * rb[part, :] * rb[part, :]
        block = x_ref[part, :].astype(F32)
        term = block * block * wide(factor, cols // lanes)
        second += jnp.sum(term.reshape(lanes // 8, 8, cols), axis=0)

    @pl.when(s < last)
    def _():
        pltpu.make_async_copy(g1r, g1r, g1_recv).wait()
        pltpu.make_async_copy(gout, gout, back_recv).wait()

    ggrad[...] = (
        jnp.sum(second + g1r[...], axis=0, keepdims=True)
        * (float(rows) ** -0.5)
        / gain_ref[:, own]
    )

    def sent(amount, semaphore):
        pltpu.make_async_copy(amount, amount, semaphore).wait()

    sent(xg.at[pl.ds(0, n_dp - 1)], xg_send)
    sent(statr.at[pl.ds(0, n_dp - 1)], st_send)

    @pl.when(s < last)
    def _():
        sent(x_ref, xp_send)
        sent(rq.at[pl.ds(0, chunks)], q_send)

    @pl.when(s == last)
    def _():
        sent(qbuf.at[:, pl.ds(0, n_dp - 1)], q_send)

    @pl.when(s > 0)
    def _():
        sent(carry, back_send)

    @pl.loop(0, groups)
    def _(g):
        part = group_rows(g)
        pltpu.make_async_copy(normed.at[part, :], normed_hbm.at[part, :], n_sem.at[g]).wait()


def chain(n_sec, n_dp, cotangent, x, scales, gain, weight):
    rows, cols = x.shape
    width = n_dp * cols
    lanes = scales.shape[1]
    chunks, groups = rows // CHUNK, rows // GROUP
    vmem = pl.BlockSpec(memory_space=pltpu.VMEM)
    hbm = pl.BlockSpec(memory_space=pl.ANY)
    sem = pltpu.SemaphoreType.DMA
    return pl.pallas_call(
        functools.partial(chain_kernel, n_sec, n_dp, rows, cols),
        name="chain",
        out_shape=(
            jax.ShapeDtypeStruct((rows, cols), BF16),
            jax.ShapeDtypeStruct((rows, cols), BF16),
            jax.ShapeDtypeStruct((1, cols), F32),
            jax.ShapeDtypeStruct(scales.shape, F32),
            jax.ShapeDtypeStruct((rows, width), BF16),
        ),
        in_specs=[vmem, vmem, vmem, vmem, hbm],
        out_specs=(vmem, vmem, vmem, vmem, hbm),
        scratch_shapes=[
            pltpu.VMEM((width, cols), BF16),
            pltpu.VMEM((cols, width), BF16),
            pltpu.VMEM((n_dp, rows, cols), BF16),
            pltpu.VMEM((rows, width), BF16),
            pltpu.VMEM((rows, cols), F32),
            pltpu.VMEM((rows, cols), BF16),
            pltpu.VMEM((rows, lanes), F32),
            pltpu.VMEM((rows, lanes), F32),
            pltpu.VMEM((2 * chunks, n_dp + 1, CHUNK, cols), BF16),
            pltpu.VMEM((chunks, n_dp, CHUNK, cols), BF16),
            pltpu.VMEM((8, cols), F32),
            pltpu.VMEM((8, cols), F32),
            pltpu.VMEM((8, lanes), F32),
            pltpu.VMEM((n_dp, 8, lanes), F32),
            sem((n_dp,)), sem, sem((groups,)), sem, sem, sem((2 * chunks,)), sem, sem, sem,
            sem, sem, sem, sem, sem((groups,)),
        ],
        compiler_params=pltpu.CompilerParams(
            collective_id=0, has_side_effects=True, vmem_limit_bytes=48 << 20
        ),
    )(cotangent, x, scales, gain, weight)


def weight_kernel(scale, normed, carry, grads, gain_grad, row_dot, w_out, g_out, gg_out, rd_out):
    w_out[...] = scale * lax.dot_general(
        normed[...], carry[...], (((0,), (0,)), ((), ())), preferred_element_type=F32
    )

    @pl.when(pl.program_id(0) == 0)
    def _():
        g_out[...] = grads[...]
        gg_out[...] = gain_grad[...]
        rd_out[...] = row_dot[...]


def weight_grads(normed, carry, grads, gain_grad, row_dot):
    rows, width = normed.shape
    cols = carry.shape[1]
    whole = lambda a: pl.BlockSpec(a.shape, lambda k: (0, 0))
    return pl.pallas_call(
        functools.partial(weight_kernel, float(rows) ** -0.5),
        name="weight_grads",
        grid=(width // cols,),
        out_shape=(
            jax.ShapeDtypeStruct((width, cols), F32),
            jax.ShapeDtypeStruct(grads.shape, grads.dtype),
            jax.ShapeDtypeStruct(gain_grad.shape, F32),
            jax.ShapeDtypeStruct(row_dot.shape, F32),
        ),
        in_specs=[
            pl.BlockSpec((rows, cols), lambda k: (0, k)),
            whole(carry), whole(grads), whole(gain_grad), whole(row_dot),
        ],
        out_specs=(
            pl.BlockSpec((cols, cols), lambda k: (k, 0)),
            whole(grads), whole(gain_grad), whole(row_dot),
        ),
        compiler_params=pltpu.CompilerParams(vmem_limit_bytes=24 << 20),
    )(normed, carry, grads, gain_grad, row_dot)


def body(n_sec, n_dp, cotangent, inputs, inv_rms, gain, weight):
    micro, per, cols = cotangent.shape
    rows = micro * per
    carry, grads, gain_grad, row_dot, normed = chain(
        n_sec, n_dp, cotangent.reshape(rows, cols), inputs.reshape(rows, cols),
        inv_rms[0], gain, weight[0],
    )
    w_grad, grads, gain_grad, row_dot = weight_grads(normed, carry, grads, gain_grad, row_dot)
    return grads.reshape(1, micro, per, cols), w_grad[None], gain_grad, row_dot[None]


def solution(mesh):
    return jax.shard_map(
        functools.partial(body, mesh.shape["section"], mesh.shape["dp"]),
        mesh=mesh,
        in_specs=(
            P(None, None, "dp"),
            P("section", None, None, "dp"),
            P("section", None, None),
            P("section", None),
            P("section", None, "dp"),
        ),
        out_specs=(
            P("section", None, None, "dp"),
            P("section", None, "dp"),
            P("section", "dp"),
            P("section", None, None),
        ),
        check_vma=False,
    )
```

```python
import functools

import jax
import jax.numpy as jnp
from jax import lax
from jax.experimental import pallas as pl
from jax.experimental.pallas import tpu as pltpu
from jax.sharding import PartitionSpec as P

MESH = pl.DeviceIdType.MESH
F32 = jnp.float32
BF16 = jnp.bfloat16
CHUNK = 16
GROUP = 64
FAR_FIRST = (5, 4, 3, 7, 2, 6, 1, 0)
BATCHES = (0, 1, 4, 8)
BACK = 4
LAG = 3
GATHERED = (1,)
PROJECTED = (1, 2, 3)
WRITES = 4
VMEM_LIMIT = 48 << 20


def wide(block, times):
    return jnp.concatenate([block] * times, axis=1)


def chain_kernel(
    sections, n_dp, rows, cols,
    cot_hbm, x_hbm, r_hbm, gain_hbm, w_hbm,
    carry_hbm, gout_hbm, ggrad, rdot, turned_hbm,
    x_ref, r_ref, gain_ref, carry, gout, turned,
    w, wt, xg, normed, u, xprev, rb, sb, rq, qbuf, g1, g1r, stat, statr,
    in_sem, w_sem, xg_send, xg_recv, xp_send, xp_recv, rq_recv, q_send, back_send, back_recv,
    g1_send, g1_recv, st_send, st_recv, out_sem,
):
    s, d = lax.axis_index("section"), lax.axis_index("dp")
    chunks, groups = rows // CHUNK, rows // GROUP
    width = n_dp * cols
    lanes = rb.shape[1]
    last = sections - 1
    nxt = jnp.minimum(s + 1, last)
    prev = jnp.maximum(s - 1, 0)

    def peer(i):
        return (d + i) % n_dp

    def partner(off):
        return d + off - 2 * sum(((d // b) % 2) * b for b in (1, 2, 4) if off & b)

    fetch = [
        pltpu.make_async_copy(x_hbm, x_ref, in_sem.at[0]),
        pltpu.make_async_copy(r_hbm, r_ref, in_sem.at[1]),
        pltpu.make_async_copy(gain_hbm, gain_ref, in_sem.at[2]),
    ]
    for copy in fetch:
        copy.start()
    first_carry = pltpu.make_async_copy(cot_hbm, carry, in_sem.at[3])

    @pl.when(s == 0)
    def _():
        first_carry.start()

    def w_copy(k):
        part = pl.ds(pl.multiple_of(k * cols, cols), cols)
        return pltpu.make_async_copy(w_hbm.at[part, :], w.at[part, :], w_sem.at[k])

    @pl.loop(0, n_dp)
    def _(k):
        w_copy(k).start()

    barrier = pltpu.get_barrier_semaphore()

    @pl.loop(1, n_dp)
    def _(i):
        pl.semaphore_signal(barrier, inc=1, device_id=(s, peer(i)), device_id_type=MESH)

    @pl.when(s > 0)
    def _():
        @pl.loop(0, n_dp)
        def _(i):
            pl.semaphore_signal(barrier, inc=1, device_id=(prev, i), device_id_type=MESH)

    @pl.when(s < last)
    def _():
        @pl.loop(0, n_dp)
        def _(i):
            pl.semaphore_signal(barrier, inc=1, device_id=(nxt, i), device_id_type=MESH)

    for copy in fetch:
        copy.wait()

    for m in range(rows // lanes):
        rb[pl.ds(m * lanes, lanes), :] = jnp.broadcast_to(r_ref[pl.ds(m, 1), :], (lanes, lanes)).T
    g1[...] = jnp.zeros_like(g1)

    @pl.when(s == last)
    def _():
        g1r[...] = jnp.zeros_like(g1r)

    inner = jnp.logical_and(s > 0, s < last)
    pl.semaphore_wait(barrier, jnp.where(inner, 3 * n_dp - 1, 2 * n_dp - 1))

    @pl.when(s < last)
    def _():
        pltpu.make_async_remote_copy(
            x_ref, xprev, xp_send, xp_recv, device_id=(nxt, d), device_id_type=MESH
        ).start()

    def group_rows(g):
        return pl.ds(pl.multiple_of(g * GROUP, GROUP), GROUP)

    def gather(g):
        part = group_rows(g)
        pltpu.make_async_copy(x_ref.at[part, :], xg.at[d, part, :], xg_recv.at[g]).start()

        @pl.loop(1, n_dp)
        def _(i):
            pltpu.make_async_remote_copy(
                x_ref.at[part, :], xg.at[d, part, :], xg_send, xg_recv.at[g],
                device_id=(s, peer(i)), device_id_type=MESH,
            ).start()

    def by_section(table):
        amount = jnp.int32(groups)
        for chip, some in reversed(list(enumerate(table))):
            amount = jnp.where(s // 2 == chip, some, amount)
        return amount

    ahead, early = by_section(GATHERED), by_section(PROJECTED)

    @pl.loop(0, ahead)
    def _(g):
        gather(g)

    @pl.loop(0, n_dp)
    def _(k):
        w_copy(k).wait()
        part = pl.ds(pl.multiple_of(k * cols, cols), cols)
        wt[:, part] = w[part, :].T

    def project(g):
        part = group_rows(g)
        pltpu.make_async_copy(xg.at[:, part, :], xg.at[:, part, :], xg_recv.at[g]).wait()
        scale = wide(rb[part, :], cols // lanes)

        @pl.loop(0, n_dp)
        def _(k):
            block = pl.ds(pl.multiple_of(k * cols, cols), cols)
            normed[part, block] = (
                xg[k, part, :].astype(F32) * scale * gain_ref[:, block]
            ).astype(BF16)

        u[part, :] = jnp.dot(normed[part, :], w[...], preferred_element_type=F32)

    @pl.loop(0, early)
    def _(g):
        project(g)

    turned_out = pltpu.make_async_copy(turned, turned_hbm, out_sem.at[0])

    def turn():
        @pl.loop(0, n_dp)
        def _(k):
            block = pl.ds(pl.multiple_of(k * cols, cols), cols)
            turned[block, :] = normed[:, block].T

        turned_out.start()

    @pl.when(early == groups)
    def _():
        turn()

    def chunk_rows(i):
        return pl.ds(pl.multiple_of(i * CHUNK, CHUNK), CHUNK)

    def total(slot):
        pltpu.make_async_copy(rq.at[slot], rq.at[slot], rq_recv.at[slot]).wait()
        added = rq[slot, 0].astype(F32)
        for k in range(1, n_dp):
            added += rq[slot, k].astype(F32)
        return added, (rq[slot, n_dp].astype(F32) + added).astype(BF16)

    def add_gain(where, x_rows, added):
        term = x_rows.astype(F32) * added
        for b in range(CHUNK // 8):
            where[...] += term[b * 8 : (b + 1) * 8, :]

    def finish(i):
        part = chunk_rows(i)
        added, result = total(chunks + i)
        gout[part, :] = result
        add_gain(g1r, x_ref[part, :], added)

    def send(i):
        part = chunk_rows(i)
        slot = jnp.where(s == last, chunks + i, i)
        mine = carry[part, :]
        scale = rb[part, :]
        row = jnp.sum(mine.astype(F32) * u[part, :], axis=1, keepdims=True) * (1.0 / width)
        row = jnp.broadcast_to(row, (CHUNK, lanes))
        sb[part, :] = row
        shift = wide(row * scale * scale, cols // lanes)
        scale = wide(scale, cols // lanes)
        qbuf[i, n_dp] = mine
        for first, end in zip(BATCHES, BATCHES[1:]):
            for o in range(first, end):
                f = partner(FAR_FIRST[o])
                block = pl.ds(pl.multiple_of(f * cols, cols), cols)
                product = jnp.dot(mine, wt[:, block], preferred_element_type=F32)
                qbuf[i, o] = (
                    product * scale * gain_ref[:, block] - xg[f, part, :].astype(F32) * shift
                ).astype(BF16)
            for o in range(first, min(end, n_dp - 1)):
                pltpu.make_async_remote_copy(
                    qbuf.at[i, o], rq.at[slot, o], q_send, rq_recv.at[slot],
                    device_id=(nxt, partner(FAR_FIRST[o])), device_id_type=MESH,
                ).start()
        own = pl.ds(n_dp - 1, 2)

        @pl.when(s < last)
        def _():
            pltpu.make_async_remote_copy(
                qbuf.at[i, own], rq.at[slot, own], q_send, rq_recv.at[slot],
                device_id=(nxt, d), device_id_type=MESH,
            ).start()

        @pl.when(s == last)
        def _():
            pltpu.make_async_copy(qbuf.at[i, own], rq.at[slot, own], rq_recv.at[slot]).start()

    def staged(i):
        per = GROUP // CHUNK
        g = i // per + 1

        @pl.when(jnp.logical_and(i % per == 0, jnp.logical_and(g >= ahead, g < groups)))
        def _():
            gather(g)

        @pl.when(jnp.logical_and(i % per == per - 1, jnp.logical_and(g >= early, g < groups)))
        def _():
            project(g)

    @pl.when(s == 0)
    def _():
        first_carry.wait()

        @pl.loop(0, chunks)
        def _(i):
            send(i)
            staged(i)

    @pl.when(s > 0)
    def _():
        pltpu.make_async_copy(xprev, xprev, xp_recv).wait()

        @pl.loop(0, chunks)
        def _(i):
            part = chunk_rows(i)
            added, result = total(i)
            carry[part, :] = result
            send(i)
            add_gain(g1, xprev[part, :], added)

            @pl.when(i % BACK == BACK - 1)
            def _():
                several = pl.ds(
                    pl.multiple_of((i - BACK + 1) * CHUNK, BACK * CHUNK), BACK * CHUNK
                )
                pltpu.make_async_remote_copy(
                    carry.at[several, :], gout.at[several, :], back_send, back_recv,
                    device_id=(prev, d), device_id_type=MESH,
                ).start()

            staged(i)

            @pl.when(jnp.logical_and(s == last, i >= LAG))
            def _():
                finish(i - LAG)

    carry_out = pltpu.make_async_copy(carry, carry_hbm, out_sem.at[1])
    carry_out.start()

    stat[...] = jnp.zeros_like(stat)
    for m in range(rows // lanes):
        stat[pl.ds(m, 1), :] = sb[pl.ds(m * lanes, lanes), :].T[0:1, :]

    pltpu.make_async_copy(stat, statr.at[d], st_recv).start()

    @pl.loop(1, n_dp)
    def _(i):
        pltpu.make_async_remote_copy(
            stat, statr.at[d], st_send, st_recv, device_id=(s, peer(i)), device_id_type=MESH
        ).start()

    @pl.when(s > 0)
    def _():
        pltpu.make_async_remote_copy(
            g1, g1r, g1_send, g1_recv, device_id=(prev, d), device_id_type=MESH
        ).start()

    @pl.when(early < groups)
    def _():
        turn()

    pltpu.make_async_copy(statr, statr, st_recv).wait()
    rows_stat = statr[0]
    for k in range(1, n_dp):
        rows_stat += statr[k]
    halves = rows // lanes
    rdot[...] = rows_stat[:halves, :] * (float(width) ** 0.5) / r_ref[...]

    own = pl.ds(pl.multiple_of(d * cols, cols), cols)
    second = jnp.zeros((8, cols), F32)
    for m in range(halves):
        part = pl.ds(m * lanes, lanes)
        column = jnp.broadcast_to(rows_stat[m : m + 1, :], (lanes, lanes)).T
        factor = column * rb[part, :] * rb[part, :]
        block = x_ref[part, :].astype(F32)
        term = block * block * wide(factor, cols // lanes)
        second += jnp.sum(term.reshape(lanes // 8, 8, cols), axis=0)

    @pl.when(s < last)
    def _():
        pltpu.make_async_copy(gout, gout, back_recv).wait()
        pltpu.make_async_copy(g1r, g1r, g1_recv).wait()

    @pl.when(s == last)
    def _():
        @pl.loop(chunks - LAG, chunks)
        def _(i):
            finish(i)

    gout_out = pltpu.make_async_copy(gout, gout_hbm, out_sem.at[2])
    gout_out.start()
    ggrad[...] = (
        jnp.sum(second + g1r[...], axis=0, keepdims=True)
        * (float(rows) ** -0.5)
        / gain_ref[:, own]
    )

    def sent(amount, semaphore):
        pltpu.make_async_copy(amount, amount, semaphore).wait()

    sent(xg.at[pl.ds(0, n_dp - 1)], xg_send)
    sent(statr.at[pl.ds(0, n_dp - 1)], st_send)

    @pl.when(s < last)
    def _():
        sent(x_ref, xp_send)
        sent(qbuf, q_send)

    @pl.when(s == last)
    def _():
        sent(qbuf.at[:, pl.ds(0, n_dp - 1)], q_send)

    @pl.when(s > 0)
    def _():
        sent(carry, back_send)
        sent(g1, g1_send)

    turned_out.wait()
    carry_out.wait()
    gout_out.wait()


def chain(n_sec, n_dp, cotangent, x, scales, gain, weight):
    rows, cols = x.shape
    width = n_dp * cols
    lanes = scales.shape[1]
    chunks, groups = rows // CHUNK, rows // GROUP
    vmem = pl.BlockSpec(memory_space=pltpu.VMEM)
    hbm = pl.BlockSpec(memory_space=pl.ANY)
    sem = pltpu.SemaphoreType.DMA
    return pl.pallas_call(
        functools.partial(chain_kernel, n_sec, n_dp, rows, cols),
        name="chain",
        out_shape=(
            jax.ShapeDtypeStruct((rows, cols), BF16),
            jax.ShapeDtypeStruct((rows, cols), BF16),
            jax.ShapeDtypeStruct((1, cols), F32),
            jax.ShapeDtypeStruct(scales.shape, F32),
            jax.ShapeDtypeStruct((width, rows), BF16),
        ),
        in_specs=[pl.BlockSpec(memory_space=pltpu.HBM)] * 5,
        out_specs=(hbm, hbm, vmem, vmem, hbm),
        scratch_shapes=[
            pltpu.VMEM((rows, cols), BF16),
            pltpu.VMEM(scales.shape, F32),
            pltpu.VMEM((1, width), F32),
            pltpu.VMEM((rows, cols), BF16),
            pltpu.VMEM((rows, cols), BF16),
            pltpu.VMEM((width, rows), BF16),
            pltpu.VMEM((width, cols), BF16),
            pltpu.VMEM((cols, width), BF16),
            pltpu.VMEM((n_dp, rows, cols), BF16),
            pltpu.VMEM((rows, width), BF16),
            pltpu.VMEM((rows, cols), F32),
            pltpu.VMEM((rows, cols), BF16),
            pltpu.VMEM((rows, lanes), F32),
            pltpu.VMEM((rows, lanes), F32),
            pltpu.VMEM((2 * chunks, n_dp + 1, CHUNK, cols), BF16),
            pltpu.VMEM((chunks, n_dp + 1, CHUNK, cols), BF16),
            pltpu.VMEM((8, cols), F32),
            pltpu.VMEM((8, cols), F32),
            pltpu.VMEM((8, lanes), F32),
            pltpu.VMEM((n_dp, 8, lanes), F32),
            sem((4,)), sem((n_dp,)), sem, sem((groups,)), sem, sem, sem((2 * chunks,)), sem, sem, sem,
            sem, sem, sem, sem, sem((3,)),
        ],
        compiler_params=pltpu.CompilerParams(
            collective_id=0, has_side_effects=True, vmem_limit_bytes=VMEM_LIMIT
        ),
    )(cotangent, x, scales, gain, weight)


def weight_kernel(scale, normed, carry, grads, gain_grad, row_dot, w_out, g_out, gg_out, rd_out):
    w_out[...] = scale * jnp.dot(normed[...], carry[...], preferred_element_type=F32)

    @pl.when(pl.program_id(0) == 0)
    def _():
        g_out[...] = grads[...]
        gg_out[...] = gain_grad[...]
        rd_out[...] = row_dot[...]


def weight_grads(normed, carry, grads, gain_grad, row_dot):
    width, rows = normed.shape
    cols = carry.shape[1]
    part = width // WRITES
    whole = lambda a: pl.BlockSpec(a.shape, lambda k: (0, 0))
    return pl.pallas_call(
        functools.partial(weight_kernel, float(rows) ** -0.5),
        name="weight_grads",
        grid=(WRITES,),
        out_shape=(
            jax.ShapeDtypeStruct((width, cols), F32),
            jax.ShapeDtypeStruct(grads.shape, grads.dtype),
            jax.ShapeDtypeStruct(gain_grad.shape, F32),
            jax.ShapeDtypeStruct(row_dot.shape, F32),
        ),
        in_specs=[
            pl.BlockSpec((part, rows), lambda k: (k, 0)),
            whole(carry), whole(grads), whole(gain_grad), whole(row_dot),
        ],
        out_specs=(
            pl.BlockSpec((part, cols), lambda k: (k, 0)),
            whole(grads), whole(gain_grad), whole(row_dot),
        ),
        compiler_params=pltpu.CompilerParams(vmem_limit_bytes=VMEM_LIMIT),
    )(normed, carry, grads, gain_grad, row_dot)


def body(n_sec, n_dp, cotangent, inputs, inv_rms, gain, weight):
    micro, per, cols = cotangent.shape
    rows = micro * per
    carry, grads, gain_grad, row_dot, normed = chain(
        n_sec, n_dp, cotangent.reshape(rows, cols), inputs.reshape(rows, cols),
        inv_rms[0], gain, weight[0],
    )
    w_grad, grads, gain_grad, row_dot = weight_grads(normed, carry, grads, gain_grad, row_dot)
    return grads.reshape(1, micro, per, cols), w_grad[None], gain_grad, row_dot[None]


def solution(mesh):
    return jax.shard_map(
        functools.partial(body, mesh.shape["section"], mesh.shape["dp"]),
        mesh=mesh,
        in_specs=(
            P(None, None, "dp"),
            P("section", None, None, "dp"),
            P("section", None, None),
            P("section", None),
            P("section", None, "dp"),
        ),
        out_specs=(
            P("section", None, None, "dp"),
            P("section", None, "dp"),
            P("section", "dp"),
            P("section", None, None),
        ),
        check_vma=False,
    )
```

```python
import functools

import jax
import jax.numpy as jnp
from jax import lax
from jax.experimental import pallas as pl
from jax.experimental.pallas import tpu as pltpu
from jax.sharding import PartitionSpec as P

MESH = pl.DeviceIdType.MESH
F32 = jnp.float32
BF16 = jnp.bfloat16
CHUNK = 16
GROUP = 64
FAR_FIRST = (5, 4, 3, 7, 2, 6, 1, 0)
BATCHES = (0, 1, 4, 8)
BACK = 4
LAG = 5
PROJECTED = (1, 3)
WRITES = 4
VMEM_LIMIT = 48 << 20


def wide(block, times):
    return jnp.concatenate([block] * times, axis=1)


def chain_kernel(
    sections, n_dp, rows, cols,
    blocks_hbm, scales_hbm, w_hbm,
    carry_hbm, gout_hbm, ggrad, rdot, turned_hbm,
    x_ref, r_ref, gain_ref, carry, gout, turned,
    w, wt, xg, normed, u, xprev, rb, sb, rq, qbuf, g1, g1r, stat, statr,
    in_sem, w_sem, xg_send, xg_recv, xp_send, xp_recv, rq_recv, q_send, back_send, back_recv,
    g1_send, g1_recv, st_send, st_recv, out_sem,
):
    s, d = lax.axis_index("section"), lax.axis_index("dp")
    chunks, groups = rows // CHUNK, rows // GROUP
    width = n_dp * cols
    lanes = rb.shape[1]
    last = sections - 1
    nxt = jnp.minimum(s + 1, last)
    prev = jnp.maximum(s - 1, 0)

    def peer(i):
        return (d + i) % n_dp

    def partner(off):
        return d + off - 2 * sum(((d // b) % 2) * b for b in (1, 2, 4) if off & b)

    fetch = [
        pltpu.make_async_copy(blocks_hbm.at[pl.ds(rows, rows), :], x_ref, in_sem.at[0]),
        pltpu.make_async_copy(scales_hbm.at[:, pl.ds(width, rows)], r_ref, in_sem.at[1]),
        pltpu.make_async_copy(scales_hbm.at[:, pl.ds(0, width)], gain_ref, in_sem.at[2]),
    ]
    for copy in fetch:
        copy.start()
    first_carry = pltpu.make_async_copy(blocks_hbm.at[pl.ds(0, rows), :], carry, in_sem.at[3])

    @pl.when(s == 0)
    def _():
        first_carry.start()

    def w_copy(k):
        part = pl.ds(pl.multiple_of(k * cols, cols), cols)
        return pltpu.make_async_copy(w_hbm.at[part, :], w.at[part, :], w_sem.at[k])

    @pl.loop(0, n_dp)
    def _(k):
        w_copy(k).start()

    barrier = pltpu.get_barrier_semaphore()

    @pl.loop(1, n_dp)
    def _(i):
        pl.semaphore_signal(barrier, inc=1, device_id=(s, peer(i)), device_id_type=MESH)

    @pl.when(s > 0)
    def _():
        @pl.loop(0, n_dp)
        def _(i):
            pl.semaphore_signal(barrier, inc=1, device_id=(prev, i), device_id_type=MESH)

    @pl.when(s < last)
    def _():
        @pl.loop(0, n_dp)
        def _(i):
            pl.semaphore_signal(barrier, inc=1, device_id=(nxt, i), device_id_type=MESH)

    for copy in fetch:
        copy.wait()

    for m in range(rows // lanes):
        rb[pl.ds(m * lanes, lanes), :] = jnp.broadcast_to(r_ref[:, pl.ds(m * lanes, lanes)], (lanes, lanes)).T
    g1[...] = jnp.zeros_like(g1)

    @pl.when(s == last)
    def _():
        g1r[...] = jnp.zeros_like(g1r)

    inner = jnp.logical_and(s > 0, s < last)
    pl.semaphore_wait(barrier, jnp.where(inner, 3 * n_dp - 1, 2 * n_dp - 1))

    @pl.when(s < last)
    def _():
        pltpu.make_async_remote_copy(
            x_ref, xprev, xp_send, xp_recv, device_id=(nxt, d), device_id_type=MESH
        ).start()

    def group_rows(g):
        return pl.ds(pl.multiple_of(g * GROUP, GROUP), GROUP)

    up, down, side = (d + 2) % n_dp, (d + n_dp - 2) % n_dp, partner(1)
    across = (d + n_dp // 2) % n_dp

    def pass_on(source, owner, part, target, semaphore):
        pltpu.make_async_remote_copy(
            source, xg.at[owner, part, :], xg_send, semaphore,
            device_id=(s, target), device_id_type=MESH,
        ).start()

    def arrived(blocks, g, semaphore):
        amount = xg.at[pl.ds(0, blocks), group_rows(g), :]
        pltpu.make_async_copy(amount, amount, semaphore).wait()

    def first_pass(g):
        part = group_rows(g)

        @pl.when(g == 0)
        def _():
            pass_on(x_ref.at[part, :], d, part, side, xg_recv.at[2, g])
            for target in (partner(5), across):
                pass_on(x_ref.at[part, :], d, part, target, xg_recv.at[0, g])

        @pl.when(g > 0)
        def _():
            pass_on(x_ref.at[part, :], d, part, side, xg_recv.at[0, g])

        pltpu.make_async_copy(x_ref.at[part, :], xg.at[d, part, :], xg_recv.at[0, g]).start()
        for target in (up, down):
            pass_on(x_ref.at[part, :], d, part, target, xg_recv.at[0, g])

    def second_pass(g):
        part = group_rows(g)

        @pl.when(g == 0)
        def _():
            arrived(1, g, xg_recv.at[2, g])

        @pl.when(g > 0)
        def _():
            arrived(4, g, xg_recv.at[0, g])
            half = GROUP // 2
            low = pl.ds(pl.multiple_of(g * GROUP, half), half)
            high = pl.ds(pl.multiple_of(g * GROUP + half, half), half)
            pass_on(xg.at[down, low, :], down, low, up, xg_recv.at[1, g])
            pass_on(xg.at[up, high, :], up, high, down, xg_recv.at[1, g])

        for target in (up, down):
            pass_on(xg.at[side, part, :], side, part, target, xg_recv.at[1, g])

    def third_pass(g):
        @pl.when(g > 0)
        def _():
            arrived(3, g, xg_recv.at[1, g])
            part = group_rows(g)
            pass_on(xg.at[across, part, :], across, part, side, xg_recv.at[2, g])

    def by_section(table):
        amount = jnp.int32(groups)
        for chip, some in reversed(list(enumerate(table))):
            amount = jnp.where(s // 2 == chip, some, amount)
        return amount

    early = by_section(PROJECTED)
    passes = ((first_pass, 2), (second_pass, 1), (third_pass, 0))

    first_pass(0)

    @pl.loop(0, n_dp)
    def _(k):
        w_copy(k).wait()
        part = pl.ds(pl.multiple_of(k * cols, cols), cols)
        wt[:, part] = w[part, :].T

    @pl.loop(1, early + 2)
    def _(k):
        for late, (one, more) in enumerate(passes):
            @pl.when(jnp.logical_and(k >= late, k - late < jnp.minimum(early + more, groups)))
            def _():
                one(k - late)

    def project(g):
        part = group_rows(g)

        @pl.when(g == 0)
        def _():
            arrived(5, g, xg_recv.at[0, g])
            arrived(2, g, xg_recv.at[1, g])

        @pl.when(g > 0)
        def _():
            arrived(1, g, xg_recv.at[2, g])

        scale = wide(rb[part, :], cols // lanes)

        @pl.loop(0, n_dp)
        def _(k):
            block = pl.ds(pl.multiple_of(k * cols, cols), cols)
            normed[part, block] = (
                xg[k, part, :].astype(F32) * scale * gain_ref[:, block]
            ).astype(BF16)

        u[part, :] = jnp.dot(normed[part, :], w[...], preferred_element_type=F32)

    @pl.loop(0, early)
    def _(g):
        project(g)

    turned_out = pltpu.make_async_copy(turned, turned_hbm, out_sem.at[0])

    def turn():
        @pl.loop(0, n_dp)
        def _(k):
            block = pl.ds(pl.multiple_of(k * cols, cols), cols)
            turned[block, :] = normed[:, block].T

        turned_out.start()

    @pl.when(early == groups)
    def _():
        turn()

    def chunk_rows(i):
        return pl.ds(pl.multiple_of(i * CHUNK, CHUNK), CHUNK)

    def total(slot):
        pltpu.make_async_copy(rq.at[slot], rq.at[slot], rq_recv.at[slot]).wait()
        added = rq[slot, 0].astype(F32)
        for k in range(1, n_dp):
            added += rq[slot, k].astype(F32)
        return added, (rq[slot, n_dp].astype(F32) + added).astype(BF16)

    def add_gain(where, x_rows, added):
        term = x_rows.astype(F32) * added
        for b in range(CHUNK // 8):
            where[...] += term[b * 8 : (b + 1) * 8, :]

    def finish(i):
        part = chunk_rows(i)
        added, result = total(chunks + i)
        gout[part, :] = result
        add_gain(g1r, x_ref[part, :], added)

    def send(i):
        part = chunk_rows(i)
        slot = jnp.where(s == last, chunks + i, i)
        mine = carry[part, :]
        scale = rb[part, :]
        row = jnp.sum(mine.astype(F32) * u[part, :], axis=1, keepdims=True) * (1.0 / width)
        row = jnp.broadcast_to(row, (CHUNK, lanes))
        sb[part, :] = row
        shift = wide(row * scale * scale, cols // lanes)
        scale = wide(scale, cols // lanes)
        qbuf[i, n_dp] = mine
        for first, end in zip(BATCHES, BATCHES[1:]):
            for o in range(first, end):
                f = partner(FAR_FIRST[o])
                block = pl.ds(pl.multiple_of(f * cols, cols), cols)
                product = jnp.dot(mine, wt[:, block], preferred_element_type=F32)
                qbuf[i, o] = (
                    product * scale * gain_ref[:, block] - xg[f, part, :].astype(F32) * shift
                ).astype(BF16)
            for o in range(first, min(end, n_dp - 1)):
                pltpu.make_async_remote_copy(
                    qbuf.at[i, o], rq.at[slot, o], q_send, rq_recv.at[slot],
                    device_id=(nxt, partner(FAR_FIRST[o])), device_id_type=MESH,
                ).start()
        own = pl.ds(n_dp - 1, 2)

        @pl.when(s < last)
        def _():
            pltpu.make_async_remote_copy(
                qbuf.at[i, own], rq.at[slot, own], q_send, rq_recv.at[slot],
                device_id=(nxt, d), device_id_type=MESH,
            ).start()

        @pl.when(s == last)
        def _():
            pltpu.make_async_copy(qbuf.at[i, own], rq.at[slot, own], rq_recv.at[slot]).start()

    def staged(i):
        per = GROUP // CHUNK
        for at, one, more in (
            (0, third_pass, 0), (1, first_pass, 2), (2, second_pass, 1), (3, project, 0)
        ):
            g = i // per + 1 + more

            @pl.when(jnp.logical_and(i % per == at, jnp.logical_and(g >= early + more, g < groups)))
            def _():
                one(g)

    @pl.when(s == 0)
    def _():
        first_carry.wait()

        @pl.loop(0, chunks)
        def _(i):
            send(i)
            staged(i)

    @pl.when(s > 0)
    def _():
        pltpu.make_async_copy(xprev, xprev, xp_recv).wait()

        @pl.loop(0, chunks)
        def _(i):
            part = chunk_rows(i)
            added, result = total(i)
            carry[part, :] = result
            send(i)
            add_gain(g1, xprev[part, :], added)

            @pl.when(i % BACK == BACK - 1)
            def _():
                several = pl.ds(
                    pl.multiple_of((i - BACK + 1) * CHUNK, BACK * CHUNK), BACK * CHUNK
                )
                pltpu.make_async_remote_copy(
                    carry.at[several, :], gout.at[several, :], back_send, back_recv,
                    device_id=(prev, d), device_id_type=MESH,
                ).start()

            staged(i)

            @pl.when(jnp.logical_and(s == last, i >= LAG))
            def _():
                finish(i - LAG)

    carry_out = pltpu.make_async_copy(carry, carry_hbm, out_sem.at[1])
    carry_out.start()

    stat[...] = jnp.zeros_like(stat)
    for m in range(rows // lanes):
        stat[pl.ds(m, 1), :] = sb[pl.ds(m * lanes, lanes), :].T[0:1, :]

    pltpu.make_async_copy(stat, statr.at[d], st_recv).start()

    @pl.loop(1, n_dp)
    def _(i):
        pltpu.make_async_remote_copy(
            stat, statr.at[d], st_send, st_recv, device_id=(s, peer(i)), device_id_type=MESH
        ).start()

    @pl.when(s > 0)
    def _():
        pltpu.make_async_remote_copy(
            g1, g1r, g1_send, g1_recv, device_id=(prev, d), device_id_type=MESH
        ).start()

    @pl.when(early < groups)
    def _():
        turn()

    pltpu.make_async_copy(statr, statr, st_recv).wait()
    rows_stat = statr[0]
    for k in range(1, n_dp):
        rows_stat += statr[k]
    halves = rows // lanes
    for m in range(halves):
        rdot[pl.ds(m, 1), :] = (
            rows_stat[m : m + 1, :] * (float(width) ** 0.5) / r_ref[:, pl.ds(m * lanes, lanes)]
        )

    own = pl.ds(pl.multiple_of(d * cols, cols), cols)
    second = jnp.zeros((8, cols), F32)
    for m in range(halves):
        part = pl.ds(m * lanes, lanes)
        column = jnp.broadcast_to(rows_stat[m : m + 1, :], (lanes, lanes)).T
        factor = column * rb[part, :] * rb[part, :]
        block = x_ref[part, :].astype(F32)
        term = block * block * wide(factor, cols // lanes)
        second += jnp.sum(term.reshape(lanes // 8, 8, cols), axis=0)

    @pl.when(s < last)
    def _():
        pltpu.make_async_copy(gout, gout, back_recv).wait()
        pltpu.make_async_copy(g1r, g1r, g1_recv).wait()

    @pl.when(s == last)
    def _():
        @pl.loop(chunks - LAG, chunks)
        def _(i):
            finish(i)

    gout_out = pltpu.make_async_copy(gout, gout_hbm, out_sem.at[2])
    gout_out.start()
    ggrad[...] = (
        jnp.sum(second + g1r[...], axis=0, keepdims=True)
        * (float(rows) ** -0.5)
        / gain_ref[:, own]
    )

    def sent(amount, semaphore):
        pltpu.make_async_copy(amount, amount, semaphore).wait()

    sent(xg.at[pl.ds(0, n_dp - 1)], xg_send)
    sent(statr.at[pl.ds(0, n_dp - 1)], st_send)

    @pl.when(s < last)
    def _():
        sent(x_ref, xp_send)
        sent(qbuf, q_send)

    @pl.when(s == last)
    def _():
        sent(qbuf.at[:, pl.ds(0, n_dp - 1)], q_send)

    @pl.when(s > 0)
    def _():
        sent(carry, back_send)
        sent(g1, g1_send)

    turned_out.wait()
    carry_out.wait()
    gout_out.wait()


def chain(n_sec, n_dp, cotangent, x, scales, gain, weight):
    rows, cols = x.shape
    width = n_dp * cols
    lanes = scales.shape[1]
    blocks = jnp.concatenate([cotangent, x], axis=0)
    factors = jnp.concatenate([gain, scales.reshape(1, rows)], axis=1)
    chunks, groups = rows // CHUNK, rows // GROUP
    vmem = pl.BlockSpec(memory_space=pltpu.VMEM)
    hbm = pl.BlockSpec(memory_space=pl.ANY)
    sem = pltpu.SemaphoreType.DMA
    return pl.pallas_call(
        functools.partial(chain_kernel, n_sec, n_dp, rows, cols),
        name="chain",
        out_shape=(
            jax.ShapeDtypeStruct((rows, cols), BF16),
            jax.ShapeDtypeStruct((rows, cols), BF16),
            jax.ShapeDtypeStruct((1, cols), F32),
            jax.ShapeDtypeStruct(scales.shape, F32),
            jax.ShapeDtypeStruct((width, rows), BF16),
        ),
        in_specs=[hbm] * 3,
        out_specs=(hbm, hbm, vmem, vmem, hbm),
        scratch_shapes=[
            pltpu.VMEM((rows, cols), BF16),
            pltpu.VMEM((1, rows), F32),
            pltpu.VMEM((1, width), F32),
            pltpu.VMEM((rows, cols), BF16),
            pltpu.VMEM((rows, cols), BF16),
            pltpu.VMEM((width, rows), BF16),
            pltpu.VMEM((width, cols), BF16),
            pltpu.VMEM((cols, width), BF16),
            pltpu.VMEM((n_dp, rows, cols), BF16),
            pltpu.VMEM((rows, width), BF16),
            pltpu.VMEM((rows, cols), F32),
            pltpu.VMEM((rows, cols), BF16),
            pltpu.VMEM((rows, lanes), F32),
            pltpu.VMEM((rows, lanes), F32),
            pltpu.VMEM((2 * chunks, n_dp + 1, CHUNK, cols), BF16),
            pltpu.VMEM((chunks, n_dp + 1, CHUNK, cols), BF16),
            pltpu.VMEM((8, cols), F32),
            pltpu.VMEM((8, cols), F32),
            pltpu.VMEM((8, lanes), F32),
            pltpu.VMEM((n_dp, 8, lanes), F32),
            sem((4,)), sem((n_dp,)), sem, sem((3, groups)), sem, sem, sem((2 * chunks,)), sem, sem, sem,
            sem, sem, sem, sem, sem((3,)),
        ],
        compiler_params=pltpu.CompilerParams(
            collective_id=0, has_side_effects=True, vmem_limit_bytes=VMEM_LIMIT
        ),
    )(blocks, factors, weight)


def weight_kernel(scale, normed, carry, grads, gain_grad, row_dot, w_out, g_out, gg_out, rd_out):
    w_out[...] = scale * jnp.dot(normed[...], carry[...], preferred_element_type=F32)

    @pl.when(pl.program_id(0) == 0)
    def _():
        g_out[...] = grads[...]
        gg_out[...] = gain_grad[...]
        rd_out[...] = row_dot[...]


def weight_grads(normed, carry, grads, gain_grad, row_dot):
    width, rows = normed.shape
    cols = carry.shape[1]
    part = width // WRITES
    whole = lambda a: pl.BlockSpec(a.shape, lambda k: (0, 0))
    return pl.pallas_call(
        functools.partial(weight_kernel, float(rows) ** -0.5),
        name="weight_grads",
        grid=(WRITES,),
        out_shape=(
            jax.ShapeDtypeStruct((width, cols), F32),
            jax.ShapeDtypeStruct(grads.shape, grads.dtype),
            jax.ShapeDtypeStruct(gain_grad.shape, F32),
            jax.ShapeDtypeStruct(row_dot.shape, F32),
        ),
        in_specs=[
            pl.BlockSpec((part, rows), lambda k: (k, 0)),
            whole(carry), whole(grads), whole(gain_grad), whole(row_dot),
        ],
        out_specs=(
            pl.BlockSpec((part, cols), lambda k: (k, 0)),
            whole(grads), whole(gain_grad), whole(row_dot),
        ),
        compiler_params=pltpu.CompilerParams(vmem_limit_bytes=VMEM_LIMIT),
    )(normed, carry, grads, gain_grad, row_dot)


def body(n_sec, n_dp, cotangent, inputs, inv_rms, gain, weight):
    micro, per, cols = cotangent.shape
    rows = micro * per
    carry, grads, gain_grad, row_dot, normed = chain(
        n_sec, n_dp, cotangent.reshape(rows, cols), inputs.reshape(rows, cols),
        inv_rms[0], gain, weight[0],
    )
    w_grad, grads, gain_grad, row_dot = weight_grads(normed, carry, grads, gain_grad, row_dot)
    return grads.reshape(1, micro, per, cols), w_grad[None], gain_grad, row_dot[None]


def solution(mesh):
    return jax.shard_map(
        functools.partial(body, mesh.shape["section"], mesh.shape["dp"]),
        mesh=mesh,
        in_specs=(
            P(None, None, "dp"),
            P("section", None, None, "dp"),
            P("section", None, None),
            P("section", None),
            P("section", None, "dp"),
        ),
        out_specs=(
            P("section", None, None, "dp"),
            P("section", None, "dp"),
            P("section", "dp"),
            P("section", None, None),
        ),
        check_vma=False,
    )
```

```python
import functools

import jax
import jax.numpy as jnp
from jax import lax
from jax.experimental import pallas as pl
from jax.experimental.pallas import tpu as pltpu
from jax.sharding import PartitionSpec as P

MESH = pl.DeviceIdType.MESH
F32 = jnp.float32
BF16 = jnp.bfloat16
CHUNK = 16
GROUP = 64
FAR_FIRST = (5, 4, 7, 3, 6, 2, 1, 0)
BATCHES = (0, 2, 4, 6, 8)
BACK = 4
LAG = 5
PROJECTED = (1, 3)
WRITES = 2
VMEM_LIMIT = 48 << 20


def wide(block, times):
    return jnp.concatenate([block] * times, axis=1)


def chain_kernel(
    sections, n_dp, rows, cols,
    blocks_hbm, scales_hbm, w_hbm,
    carry_hbm, gout_hbm, ggrad, rdot, turned_hbm,
    x_ref, r_ref, gain_ref, carry, gout, turned,
    w, wt, xg, normed, u, xprev, rb, sb, rq, qbuf, g1, g1r, stat, statr,
    in_sem, w_sem, xg_send, xg_recv, xp_send, xp_recv, rq_recv, q_send, back_send, back_recv,
    g1_send, g1_recv, st_send, st_recv, out_sem,
):
    s, d = lax.axis_index("section"), lax.axis_index("dp")
    chunks, groups = rows // CHUNK, rows // GROUP
    width = n_dp * cols
    lanes = rb.shape[1]
    last = sections - 1
    nxt = jnp.minimum(s + 1, last)
    prev = jnp.maximum(s - 1, 0)

    def peer(i):
        return (d + i) % n_dp

    def partner(off):
        return d + off - 2 * sum(((d // b) % 2) * b for b in (1, 2, 4) if off & b)

    fetch = [
        pltpu.make_async_copy(blocks_hbm.at[pl.ds(rows, rows), :], x_ref, in_sem.at[0]),
        pltpu.make_async_copy(scales_hbm.at[:, pl.ds(width, rows)], r_ref, in_sem.at[1]),
        pltpu.make_async_copy(scales_hbm.at[:, pl.ds(0, width)], gain_ref, in_sem.at[2]),
    ]
    for copy in fetch:
        copy.start()
    first_carry = pltpu.make_async_copy(blocks_hbm.at[pl.ds(0, rows), :], carry, in_sem.at[3])

    @pl.when(s == 0)
    def _():
        first_carry.start()

    def w_copy(k):
        part = pl.ds(pl.multiple_of(k * cols, cols), cols)
        return pltpu.make_async_copy(w_hbm.at[part, :], w.at[part, :], w_sem.at[k])

    @pl.loop(0, n_dp)
    def _(k):
        w_copy(k).start()

    barrier = pltpu.get_barrier_semaphore()

    @pl.loop(1, n_dp)
    def _(i):
        pl.semaphore_signal(barrier, inc=1, device_id=(s, peer(i)), device_id_type=MESH)

    @pl.when(s > 0)
    def _():
        @pl.loop(0, n_dp)
        def _(i):
            pl.semaphore_signal(barrier, inc=1, device_id=(prev, i), device_id_type=MESH)

    @pl.when(s < last)
    def _():
        @pl.loop(0, n_dp)
        def _(i):
            pl.semaphore_signal(barrier, inc=1, device_id=(nxt, i), device_id_type=MESH)

    for copy in fetch:
        copy.wait()

    for m in range(rows // lanes):
        rb[pl.ds(m * lanes, lanes), :] = jnp.broadcast_to(r_ref[:, pl.ds(m * lanes, lanes)], (lanes, lanes)).T
    g1[...] = jnp.zeros_like(g1)

    @pl.when(s == last)
    def _():
        g1r[...] = jnp.zeros_like(g1r)

    inner = jnp.logical_and(s > 0, s < last)
    pl.semaphore_wait(barrier, jnp.where(inner, 3 * n_dp - 1, 2 * n_dp - 1))

    @pl.when(s < last)
    def _():
        pltpu.make_async_remote_copy(
            x_ref, xprev, xp_send, xp_recv, device_id=(nxt, d), device_id_type=MESH
        ).start()

    def group_rows(g):
        return pl.ds(pl.multiple_of(g * GROUP, GROUP), GROUP)

    up, down, side = (d + 2) % n_dp, (d + n_dp - 2) % n_dp, partner(1)
    across = (d + n_dp // 2) % n_dp

    def pass_on(source, owner, part, target, semaphore):
        pltpu.make_async_remote_copy(
            source, xg.at[owner, part, :], xg_send, semaphore,
            device_id=(s, target), device_id_type=MESH,
        ).start()

    def arrived(blocks, g, semaphore):
        amount = xg.at[pl.ds(0, blocks), group_rows(g), :]
        pltpu.make_async_copy(amount, amount, semaphore).wait()

    def first_pass(g):
        part = group_rows(g)

        @pl.when(g == 0)
        def _():
            pass_on(x_ref.at[part, :], d, part, side, xg_recv.at[2, g])
            for target in (partner(5), across):
                pass_on(x_ref.at[part, :], d, part, target, xg_recv.at[0, g])

        @pl.when(g > 0)
        def _():
            pass_on(x_ref.at[part, :], d, part, side, xg_recv.at[0, g])

        pltpu.make_async_copy(x_ref.at[part, :], xg.at[d, part, :], xg_recv.at[0, g]).start()
        for target in (up, down):
            pass_on(x_ref.at[part, :], d, part, target, xg_recv.at[0, g])

    def second_pass(g):
        part = group_rows(g)

        @pl.when(g == 0)
        def _():
            arrived(1, g, xg_recv.at[2, g])

        @pl.when(g > 0)
        def _():
            arrived(4, g, xg_recv.at[0, g])
            half = GROUP // 2
            low = pl.ds(pl.multiple_of(g * GROUP, half), half)
            high = pl.ds(pl.multiple_of(g * GROUP + half, half), half)
            pass_on(xg.at[down, low, :], down, low, up, xg_recv.at[1, g])
            pass_on(xg.at[up, high, :], up, high, down, xg_recv.at[1, g])

        for target in (up, down):
            pass_on(xg.at[side, part, :], side, part, target, xg_recv.at[1, g])

    def third_pass(g):
        @pl.when(g > 0)
        def _():
            arrived(3, g, xg_recv.at[1, g])
            part = group_rows(g)
            pass_on(xg.at[across, part, :], across, part, side, xg_recv.at[2, g])

    def by_section(table):
        amount = jnp.int32(groups)
        for chip, some in reversed(list(enumerate(table))):
            amount = jnp.where(s // 2 == chip, some, amount)
        return amount

    early = by_section(PROJECTED)
    passes = ((first_pass, 2), (second_pass, 1), (third_pass, 0))

    first_pass(0)

    @pl.loop(0, n_dp)
    def _(k):
        w_copy(k).wait()
        part = pl.ds(pl.multiple_of(k * cols, cols), cols)
        wt[:, part] = w[part, :].T

    @pl.loop(1, early + 2)
    def _(k):
        for late, (one, more) in enumerate(passes):
            @pl.when(jnp.logical_and(k >= late, k - late < jnp.minimum(early + more, groups)))
            def _():
                one(k - late)

    def project(g):
        part = group_rows(g)

        @pl.when(g == 0)
        def _():
            arrived(5, g, xg_recv.at[0, g])
            arrived(2, g, xg_recv.at[1, g])

        @pl.when(g > 0)
        def _():
            arrived(1, g, xg_recv.at[2, g])

        scale = wide(rb[part, :], cols // lanes)

        @pl.loop(0, n_dp)
        def _(k):
            block = pl.ds(pl.multiple_of(k * cols, cols), cols)
            normed[part, block] = (
                xg[k, part, :].astype(F32) * scale * gain_ref[:, block]
            ).astype(BF16)

        u[part, :] = jnp.dot(normed[part, :], w[...], preferred_element_type=F32)

    @pl.loop(0, early)
    def _(g):
        project(g)

    turned_out = pltpu.make_async_copy(turned, turned_hbm, out_sem.at[0])

    def turn():
        @pl.loop(0, n_dp)
        def _(k):
            block = pl.ds(pl.multiple_of(k * cols, cols), cols)
            turned[block, :] = normed[:, block].T

        turned_out.start()

    @pl.when(early == groups)
    def _():
        turn()

    def chunk_rows(i):
        return pl.ds(pl.multiple_of(i * CHUNK, CHUNK), CHUNK)

    def total(slot):
        pltpu.make_async_copy(rq.at[slot], rq.at[slot], rq_recv.at[slot]).wait()
        added = rq[slot, 0].astype(F32)
        for k in range(1, n_dp):
            added += rq[slot, k].astype(F32)
        return added, (rq[slot, n_dp].astype(F32) + added).astype(BF16)

    def add_gain(where, x_rows, added):
        term = x_rows.astype(F32) * added
        for b in range(CHUNK // 8):
            where[...] += term[b * 8 : (b + 1) * 8, :]

    def finish(i):
        part = chunk_rows(i)
        added, result = total(chunks + i)
        gout[part, :] = result
        add_gain(g1r, x_ref[part, :], added)

    def send(i):
        part = chunk_rows(i)
        slot = jnp.where(s == last, chunks + i, i)
        mine = carry[part, :]
        scale = rb[part, :]
        row = jnp.sum(mine.astype(F32) * u[part, :], axis=1, keepdims=True) * (1.0 / width)
        row = jnp.broadcast_to(row, (CHUNK, lanes))
        sb[part, :] = row
        shift = wide(row * scale * scale, cols // lanes)
        scale = wide(scale, cols // lanes)
        qbuf[i, n_dp] = mine
        for first, end in zip(BATCHES, BATCHES[1:]):
            for o in range(first, end):
                f = partner(FAR_FIRST[o])
                block = pl.ds(pl.multiple_of(f * cols, cols), cols)
                product = jnp.dot(mine, wt[:, block], preferred_element_type=F32)
                qbuf[i, o] = (
                    product * scale * gain_ref[:, block] - xg[f, part, :].astype(F32) * shift
                ).astype(BF16)
            for o in range(first, min(end, n_dp - 1)):
                pltpu.make_async_remote_copy(
                    qbuf.at[i, o], rq.at[slot, o], q_send, rq_recv.at[slot],
                    device_id=(nxt, partner(FAR_FIRST[o])), device_id_type=MESH,
                ).start()
        own = pl.ds(n_dp - 1, 2)

        @pl.when(s < last)
        def _():
            pltpu.make_async_remote_copy(
                qbuf.at[i, own], rq.at[slot, own], q_send, rq_recv.at[slot],
                device_id=(nxt, d), device_id_type=MESH,
            ).start()

        @pl.when(s == last)
        def _():
            pltpu.make_async_copy(qbuf.at[i, own], rq.at[slot, own], rq_recv.at[slot]).start()

    def staged(i):
        per = GROUP // CHUNK
        for at, one, more in (
            (0, third_pass, 0), (1, first_pass, 2), (2, second_pass, 1), (3, project, 0)
        ):
            g = i // per + 1 + more

            @pl.when(jnp.logical_and(i % per == at, jnp.logical_and(g >= early + more, g < groups)))
            def _():
                one(g)

    @pl.when(s == 0)
    def _():
        first_carry.wait()

        @pl.loop(0, chunks)
        def _(i):
            send(i)
            staged(i)

    @pl.when(s > 0)
    def _():
        pltpu.make_async_copy(xprev, xprev, xp_recv).wait()

        @pl.loop(0, chunks)
        def _(i):
            part = chunk_rows(i)
            added, result = total(i)
            carry[part, :] = result
            send(i)
            add_gain(g1, xprev[part, :], added)

            @pl.when(i % BACK == BACK - 1)
            def _():
                several = pl.ds(
                    pl.multiple_of((i - BACK + 1) * CHUNK, BACK * CHUNK), BACK * CHUNK
                )
                pltpu.make_async_remote_copy(
                    carry.at[several, :], gout.at[several, :], back_send, back_recv,
                    device_id=(prev, d), device_id_type=MESH,
                ).start()

            staged(i)

            @pl.when(jnp.logical_and(s == last, i >= LAG))
            def _():
                finish(i - LAG)

    carry_out = pltpu.make_async_copy(carry, carry_hbm, out_sem.at[1])
    carry_out.start()

    stat[...] = jnp.zeros_like(stat)
    for m in range(rows // lanes):
        stat[pl.ds(m, 1), :] = sb[pl.ds(m * lanes, lanes), :].T[0:1, :]

    pltpu.make_async_copy(stat, statr.at[d], st_recv).start()

    @pl.loop(1, n_dp)
    def _(i):
        pltpu.make_async_remote_copy(
            stat, statr.at[d], st_send, st_recv, device_id=(s, peer(i)), device_id_type=MESH
        ).start()

    @pl.when(s > 0)
    def _():
        pltpu.make_async_remote_copy(
            g1, g1r, g1_send, g1_recv, device_id=(prev, d), device_id_type=MESH
        ).start()

    @pl.when(early < groups)
    def _():
        turn()

    pltpu.make_async_copy(statr, statr, st_recv).wait()
    rows_stat = statr[0]
    for k in range(1, n_dp):
        rows_stat += statr[k]
    halves = rows // lanes
    for m in range(halves):
        rdot[pl.ds(m, 1), :] = (
            rows_stat[m : m + 1, :] * (float(width) ** 0.5) / r_ref[:, pl.ds(m * lanes, lanes)]
        )

    own = pl.ds(pl.multiple_of(d * cols, cols), cols)
    second = jnp.zeros((8, cols), F32)
    for m in range(halves):
        part = pl.ds(m * lanes, lanes)
        column = jnp.broadcast_to(rows_stat[m : m + 1, :], (lanes, lanes)).T
        factor = column * rb[part, :] * rb[part, :]
        block = x_ref[part, :].astype(F32)
        term = block * block * wide(factor, cols // lanes)
        second += jnp.sum(term.reshape(lanes // 8, 8, cols), axis=0)

    @pl.when(s < last)
    def _():
        pltpu.make_async_copy(gout, gout, back_recv).wait()
        pltpu.make_async_copy(g1r, g1r, g1_recv).wait()

    @pl.when(s == last)
    def _():
        @pl.loop(chunks - LAG, chunks)
        def _(i):
            finish(i)

    gout_out = pltpu.make_async_copy(gout, gout_hbm, out_sem.at[2])
    gout_out.start()
    ggrad[...] = (
        jnp.sum(second + g1r[...], axis=0, keepdims=True)
        * (float(rows) ** -0.5)
        / gain_ref[:, own]
    )

    def sent(amount, semaphore):
        pltpu.make_async_copy(amount, amount, semaphore).wait()

    sent(xg.at[pl.ds(0, n_dp - 1)], xg_send)
    sent(statr.at[pl.ds(0, n_dp - 1)], st_send)

    @pl.when(s < last)
    def _():
        sent(x_ref, xp_send)
        sent(qbuf, q_send)

    @pl.when(s == last)
    def _():
        sent(qbuf.at[:, pl.ds(0, n_dp - 1)], q_send)

    @pl.when(s > 0)
    def _():
        sent(carry, back_send)
        sent(g1, g1_send)

    turned_out.wait()
    carry_out.wait()
    gout_out.wait()


def chain(n_sec, n_dp, cotangent, x, scales, gain, weight):
    rows, cols = x.shape
    width = n_dp * cols
    lanes = scales.shape[1]
    blocks = jnp.concatenate([cotangent, x], axis=0)
    factors = jnp.concatenate([gain, scales.reshape(1, rows)], axis=1)
    chunks, groups = rows // CHUNK, rows // GROUP
    vmem = pl.BlockSpec(memory_space=pltpu.VMEM)
    hbm = pl.BlockSpec(memory_space=pl.ANY)
    sem = pltpu.SemaphoreType.DMA
    return pl.pallas_call(
        functools.partial(chain_kernel, n_sec, n_dp, rows, cols),
        name="chain",
        out_shape=(
            jax.ShapeDtypeStruct((rows, cols), BF16),
            jax.ShapeDtypeStruct((rows, cols), BF16),
            jax.ShapeDtypeStruct((1, cols), F32),
            jax.ShapeDtypeStruct(scales.shape, F32),
            jax.ShapeDtypeStruct((width, rows), BF16),
        ),
        in_specs=[hbm] * 3,
        out_specs=(hbm, hbm, vmem, vmem, hbm),
        scratch_shapes=[
            pltpu.VMEM((rows, cols), BF16),
            pltpu.VMEM((1, rows), F32),
            pltpu.VMEM((1, width), F32),
            pltpu.VMEM((rows, cols), BF16),
            pltpu.VMEM((rows, cols), BF16),
            pltpu.VMEM((width, rows), BF16),
            pltpu.VMEM((width, cols), BF16),
            pltpu.VMEM((cols, width), BF16),
            pltpu.VMEM((n_dp, rows, cols), BF16),
            pltpu.VMEM((rows, width), BF16),
            pltpu.VMEM((rows, cols), F32),
            pltpu.VMEM((rows, cols), BF16),
            pltpu.VMEM((rows, lanes), F32),
            pltpu.VMEM((rows, lanes), F32),
            pltpu.VMEM((2 * chunks, n_dp + 1, CHUNK, cols), BF16),
            pltpu.VMEM((chunks, n_dp + 1, CHUNK, cols), BF16),
            pltpu.VMEM((8, cols), F32),
            pltpu.VMEM((8, cols), F32),
            pltpu.VMEM((8, lanes), F32),
            pltpu.VMEM((n_dp, 8, lanes), F32),
            sem((4,)), sem((n_dp,)), sem, sem((3, groups)), sem, sem, sem((2 * chunks,)), sem, sem, sem,
            sem, sem, sem, sem, sem((3,)),
        ],
        compiler_params=pltpu.CompilerParams(
            collective_id=0, has_side_effects=True, vmem_limit_bytes=VMEM_LIMIT
        ),
    )(blocks, factors, weight)


def weight_kernel(scale, normed, carry, grads, gain_grad, row_dot, w_out, g_out, gg_out, rd_out):
    w_out[...] = scale * jnp.dot(normed[...], carry[...], preferred_element_type=F32)

    @pl.when(pl.program_id(0) == 0)
    def _():
        g_out[...] = grads[...]
        gg_out[...] = gain_grad[...]
        rd_out[...] = row_dot[...]


def weight_grads(normed, carry, grads, gain_grad, row_dot):
    width, rows = normed.shape
    cols = carry.shape[1]
    part = width // WRITES
    whole = lambda a: pl.BlockSpec(a.shape, lambda k: (0, 0))
    return pl.pallas_call(
        functools.partial(weight_kernel, float(rows) ** -0.5),
        name="weight_grads",
        grid=(WRITES,),
        out_shape=(
            jax.ShapeDtypeStruct((width, cols), F32),
            jax.ShapeDtypeStruct(grads.shape, grads.dtype),
            jax.ShapeDtypeStruct(gain_grad.shape, F32),
            jax.ShapeDtypeStruct(row_dot.shape, F32),
        ),
        in_specs=[
            pl.BlockSpec((part, rows), lambda k: (k, 0)),
            whole(carry), whole(grads), whole(gain_grad), whole(row_dot),
        ],
        out_specs=(
            pl.BlockSpec((part, cols), lambda k: (k, 0)),
            whole(grads), whole(gain_grad), whole(row_dot),
        ),
        compiler_params=pltpu.CompilerParams(vmem_limit_bytes=VMEM_LIMIT),
    )(normed, carry, grads, gain_grad, row_dot)


def body(n_sec, n_dp, cotangent, inputs, inv_rms, gain, weight):
    micro, per, cols = cotangent.shape
    rows = micro * per
    carry, grads, gain_grad, row_dot, normed = chain(
        n_sec, n_dp, cotangent.reshape(rows, cols), inputs.reshape(rows, cols),
        inv_rms[0], gain, weight[0],
    )
    w_grad, grads, gain_grad, row_dot = weight_grads(normed, carry, grads, gain_grad, row_dot)
    return grads.reshape(1, micro, per, cols), w_grad[None], gain_grad, row_dot[None]


def solution(mesh):
    return jax.shard_map(
        functools.partial(body, mesh.shape["section"], mesh.shape["dp"]),
        mesh=mesh,
        in_specs=(
            P(None, None, "dp"),
            P("section", None, None, "dp"),
            P("section", None, None),
            P("section", None),
            P("section", None, "dp"),
        ),
        out_specs=(
            P("section", None, None, "dp"),
            P("section", None, "dp"),
            P("section", "dp"),
            P("section", None, None),
        ),
        check_vma=False,
    )
```

```python
import functools

import jax
import jax.numpy as jnp
from jax import lax
from jax.experimental import pallas as pl
from jax.experimental.pallas import tpu as pltpu
from jax.sharding import PartitionSpec as P

MESH = pl.DeviceIdType.MESH
F32 = jnp.float32
BF16 = jnp.bfloat16
CHUNK = 16
GROUP = 64
FAR_FIRST = (5, 4, 7, 3, 6, 2, 1, 0)
BATCHES = (0, 2, 5, 8)
BACK = 4
LAG = 5
PROJECTED = (1, 2, 3)
WRITES = 2
VMEM_LIMIT = 48 << 20


def wide(block, times):
    return jnp.concatenate([block] * times, axis=1)


def chain_kernel(
    sections, n_dp, rows, cols,
    blocks_hbm, scales_hbm, w_hbm,
    carry_hbm, gout_hbm, ggrad, rdot, turned_hbm,
    x_ref, r_ref, gain_ref, carry, gout, turned,
    w, wt, xg, normed, u, xprev, rb, sb, rq, qbuf, g1, g1r, stat, statr,
    in_sem, w_sem, xg_send, xg_recv, xp_send, xp_recv, rq_recv, q_send, back_send, back_recv,
    g1_send, g1_recv, st_send, st_recv, out_sem,
):
    s, d = lax.axis_index("section"), lax.axis_index("dp")
    chunks, groups = rows // CHUNK, rows // GROUP
    width = n_dp * cols
    lanes = rb.shape[1]
    last = sections - 1
    nxt = jnp.minimum(s + 1, last)
    prev = jnp.maximum(s - 1, 0)

    def peer(i):
        return (d + i) % n_dp

    def partner(off):
        return d + off - 2 * sum(((d // b) % 2) * b for b in (1, 2, 4) if off & b)

    fetch = [
        pltpu.make_async_copy(blocks_hbm.at[pl.ds(rows, rows), :], x_ref, in_sem.at[0]),
        pltpu.make_async_copy(scales_hbm.at[:, pl.ds(width, rows)], r_ref, in_sem.at[1]),
        pltpu.make_async_copy(scales_hbm.at[:, pl.ds(0, width)], gain_ref, in_sem.at[2]),
    ]
    for copy in fetch:
        copy.start()
    first_carry = pltpu.make_async_copy(blocks_hbm.at[pl.ds(0, rows), :], carry, in_sem.at[3])

    @pl.when(s == 0)
    def _():
        first_carry.start()

    def w_copy(k):
        part = pl.ds(pl.multiple_of(k * cols, cols), cols)
        return pltpu.make_async_copy(w_hbm.at[part, :], w.at[part, :], w_sem.at[k])

    @pl.loop(0, n_dp)
    def _(k):
        w_copy(k).start()

    barrier = pltpu.get_barrier_semaphore()

    @pl.loop(1, n_dp)
    def _(i):
        pl.semaphore_signal(barrier, inc=1, device_id=(s, peer(i)), device_id_type=MESH)

    @pl.when(s > 0)
    def _():
        @pl.loop(0, n_dp)
        def _(i):
            pl.semaphore_signal(barrier, inc=1, device_id=(prev, i), device_id_type=MESH)

    @pl.when(s < last)
    def _():
        @pl.loop(0, n_dp)
        def _(i):
            pl.semaphore_signal(barrier, inc=1, device_id=(nxt, i), device_id_type=MESH)

    for copy in fetch:
        copy.wait()

    for m in range(rows // lanes):
        rb[pl.ds(m * lanes, lanes), :] = jnp.broadcast_to(r_ref[:, pl.ds(m * lanes, lanes)], (lanes, lanes)).T
    g1[...] = jnp.zeros_like(g1)

    @pl.when(s == last)
    def _():
        g1r[...] = jnp.zeros_like(g1r)

    inner = jnp.logical_and(s > 0, s < last)
    pl.semaphore_wait(barrier, jnp.where(inner, 3 * n_dp - 1, 2 * n_dp - 1))

    @pl.when(s < last)
    def _():
        pltpu.make_async_remote_copy(
            x_ref, xprev, xp_send, xp_recv, device_id=(nxt, d), device_id_type=MESH
        ).start()

    def group_rows(g):
        return pl.ds(pl.multiple_of(g * GROUP, GROUP), GROUP)

    up, down, side = (d + 2) % n_dp, (d + n_dp - 2) % n_dp, partner(1)
    across = (d + n_dp // 2) % n_dp

    def pass_on(source, owner, part, target, semaphore):
        pltpu.make_async_remote_copy(
            source, xg.at[owner, part, :], xg_send, semaphore,
            device_id=(s, target), device_id_type=MESH,
        ).start()

    def arrived(blocks, g, semaphore):
        amount = xg.at[pl.ds(0, blocks), group_rows(g), :]
        pltpu.make_async_copy(amount, amount, semaphore).wait()

    def first_pass(g):
        part = group_rows(g)

        @pl.when(g == 0)
        def _():
            pass_on(x_ref.at[part, :], d, part, side, xg_recv.at[2, g])
            for target in (partner(5), across):
                pass_on(x_ref.at[part, :], d, part, target, xg_recv.at[0, g])

        @pl.when(g > 0)
        def _():
            pass_on(x_ref.at[part, :], d, part, side, xg_recv.at[0, g])

        pltpu.make_async_copy(x_ref.at[part, :], xg.at[d, part, :], xg_recv.at[0, g]).start()
        for target in (up, down):
            pass_on(x_ref.at[part, :], d, part, target, xg_recv.at[0, g])

    def second_pass(g):
        part = group_rows(g)

        @pl.when(g == 0)
        def _():
            arrived(1, g, xg_recv.at[2, g])

        @pl.when(g > 0)
        def _():
            arrived(4, g, xg_recv.at[0, g])
            half = GROUP // 2
            low = pl.ds(pl.multiple_of(g * GROUP, half), half)
            high = pl.ds(pl.multiple_of(g * GROUP + half, half), half)
            pass_on(xg.at[down, low, :], down, low, up, xg_recv.at[1, g])
            pass_on(xg.at[up, high, :], up, high, down, xg_recv.at[1, g])

        for target in (up, down):
            pass_on(xg.at[side, part, :], side, part, target, xg_recv.at[1, g])

    def third_pass(g):
        @pl.when(g > 0)
        def _():
            arrived(3, g, xg_recv.at[1, g])
            part = group_rows(g)
            pass_on(xg.at[across, part, :], across, part, side, xg_recv.at[2, g])

    def by_section(table):
        amount = jnp.int32(groups)
        for chip, some in reversed(list(enumerate(table))):
            amount = jnp.where(s // 2 == chip, some, amount)
        return amount

    early = by_section(PROJECTED)
    passes = ((first_pass, 2), (second_pass, 1), (third_pass, 0))

    first_pass(0)

    @pl.loop(0, n_dp)
    def _(k):
        w_copy(k).wait()
        part = pl.ds(pl.multiple_of(k * cols, cols), cols)
        wt[:, part] = w[part, :].T

    @pl.loop(1, early + 2)
    def _(k):
        for late, (one, more) in enumerate(passes):
            @pl.when(jnp.logical_and(k >= late, k - late < jnp.minimum(early + more, groups)))
            def _():
                one(k - late)

    def project(g):
        part = group_rows(g)

        @pl.when(g == 0)
        def _():
            arrived(5, g, xg_recv.at[0, g])
            arrived(2, g, xg_recv.at[1, g])

        @pl.when(g > 0)
        def _():
            arrived(1, g, xg_recv.at[2, g])

        scale = wide(rb[part, :], cols // lanes)

        @pl.loop(0, n_dp)
        def _(k):
            block = pl.ds(pl.multiple_of(k * cols, cols), cols)
            normed[part, block] = (
                xg[k, part, :].astype(F32) * scale * gain_ref[:, block]
            ).astype(BF16)

        u[part, :] = jnp.dot(normed[part, :], w[...], preferred_element_type=F32)

    @pl.loop(0, early)
    def _(g):
        project(g)

    turned_out = pltpu.make_async_copy(turned, turned_hbm, out_sem.at[0])

    def turn():
        @pl.loop(0, n_dp)
        def _(k):
            block = pl.ds(pl.multiple_of(k * cols, cols), cols)
            turned[block, :] = normed[:, block].T

        turned_out.start()

    @pl.when(early == groups)
    def _():
        turn()

    def chunk_rows(i):
        return pl.ds(pl.multiple_of(i * CHUNK, CHUNK), CHUNK)

    def total(slot):
        pltpu.make_async_copy(rq.at[slot], rq.at[slot], rq_recv.at[slot]).wait()
        added = rq[slot, 0].astype(F32)
        for k in range(1, n_dp):
            added += rq[slot, k].astype(F32)
        return added, (rq[slot, n_dp].astype(F32) + added).astype(BF16)

    def add_gain(where, x_rows, added):
        term = x_rows.astype(F32) * added
        for b in range(CHUNK // 8):
            where[...] += term[b * 8 : (b + 1) * 8, :]

    def finish(i):
        part = chunk_rows(i)
        added, result = total(chunks + i)
        gout[part, :] = result
        add_gain(g1r, x_ref[part, :], added)

    def send(i):
        part = chunk_rows(i)
        slot = jnp.where(s == last, chunks + i, i)
        mine = carry[part, :]
        scale = rb[part, :]
        row = jnp.sum(mine.astype(F32) * u[part, :], axis=1, keepdims=True) * (1.0 / width)
        row = jnp.broadcast_to(row, (CHUNK, lanes))
        sb[part, :] = row
        shift = wide(row * scale * scale, cols // lanes)
        scale = wide(scale, cols // lanes)
        qbuf[i, n_dp] = mine
        for first, end in zip(BATCHES, BATCHES[1:]):
            for o in range(first, end):
                f = partner(FAR_FIRST[o])
                block = pl.ds(pl.multiple_of(f * cols, cols), cols)
                product = jnp.dot(mine, wt[:, block], preferred_element_type=F32)
                qbuf[i, o] = (
                    product * scale * gain_ref[:, block] - xg[f, part, :].astype(F32) * shift
                ).astype(BF16)
            for o in range(first, min(end, n_dp - 1)):
                pltpu.make_async_remote_copy(
                    qbuf.at[i, o], rq.at[slot, o], q_send, rq_recv.at[slot],
                    device_id=(nxt, partner(FAR_FIRST[o])), device_id_type=MESH,
                ).start()
        own = pl.ds(n_dp - 1, 2)

        @pl.when(s < last)
        def _():
            pltpu.make_async_remote_copy(
                qbuf.at[i, own], rq.at[slot, own], q_send, rq_recv.at[slot],
                device_id=(nxt, d), device_id_type=MESH,
            ).start()

        @pl.when(s == last)
        def _():
            pltpu.make_async_copy(qbuf.at[i, own], rq.at[slot, own], rq_recv.at[slot]).start()

    def staged(i):
        per = GROUP // CHUNK
        for at, one, more in (
            (0, third_pass, 0), (1, first_pass, 2), (2, second_pass, 1), (3, project, 0)
        ):
            g = i // per + 1 + more

            @pl.when(jnp.logical_and(i % per == at, jnp.logical_and(g >= early + more, g < groups)))
            def _():
                one(g)

    @pl.when(s == 0)
    def _():
        first_carry.wait()

        @pl.loop(0, chunks)
        def _(i):
            send(i)
            staged(i)

    @pl.when(s > 0)
    def _():
        pltpu.make_async_copy(xprev, xprev, xp_recv).wait()

        @pl.loop(0, chunks)
        def _(i):
            part = chunk_rows(i)
            added, result = total(i)
            carry[part, :] = result
            send(i)
            add_gain(g1, xprev[part, :], added)

            @pl.when(i % BACK == BACK - 1)
            def _():
                several = pl.ds(
                    pl.multiple_of((i - BACK + 1) * CHUNK, BACK * CHUNK), BACK * CHUNK
                )
                pltpu.make_async_remote_copy(
                    carry.at[several, :], gout.at[several, :], back_send, back_recv,
                    device_id=(prev, d), device_id_type=MESH,
                ).start()

            staged(i)

            @pl.when(jnp.logical_and(s == last, i >= LAG))
            def _():
                finish(i - LAG)

    carry_out = pltpu.make_async_copy(carry, carry_hbm, out_sem.at[1])
    carry_out.start()

    stat[...] = jnp.zeros_like(stat)
    for m in range(rows // lanes):
        stat[pl.ds(m, 1), :] = sb[pl.ds(m * lanes, lanes), :].T[0:1, :]

    pltpu.make_async_copy(stat, statr.at[d], st_recv).start()

    @pl.loop(1, n_dp)
    def _(i):
        pltpu.make_async_remote_copy(
            stat, statr.at[d], st_send, st_recv, device_id=(s, peer(i)), device_id_type=MESH
        ).start()

    @pl.when(s > 0)
    def _():
        pltpu.make_async_remote_copy(
            g1, g1r, g1_send, g1_recv, device_id=(prev, d), device_id_type=MESH
        ).start()

    @pl.when(early < groups)
    def _():
        turn()

    pltpu.make_async_copy(statr, statr, st_recv).wait()
    rows_stat = statr[0]
    for k in range(1, n_dp):
        rows_stat += statr[k]
    halves = rows // lanes
    for m in range(halves):
        rdot[pl.ds(m, 1), :] = (
            rows_stat[m : m + 1, :] * (float(width) ** 0.5) / r_ref[:, pl.ds(m * lanes, lanes)]
        )

    own = pl.ds(pl.multiple_of(d * cols, cols), cols)
    second = jnp.zeros((8, cols), F32)
    for m in range(halves):
        part = pl.ds(m * lanes, lanes)
        column = jnp.broadcast_to(rows_stat[m : m + 1, :], (lanes, lanes)).T
        factor = column * rb[part, :] * rb[part, :]
        block = x_ref[part, :].astype(F32)
        term = block * block * wide(factor, cols // lanes)
        second += jnp.sum(term.reshape(lanes // 8, 8, cols), axis=0)

    @pl.when(s < last)
    def _():
        pltpu.make_async_copy(gout, gout, back_recv).wait()
        pltpu.make_async_copy(g1r, g1r, g1_recv).wait()

    @pl.when(s == last)
    def _():
        @pl.loop(chunks - LAG, chunks)
        def _(i):
            finish(i)

    gout_out = pltpu.make_async_copy(gout, gout_hbm, out_sem.at[2])
    gout_out.start()
    ggrad[...] = (
        jnp.sum(second + g1r[...], axis=0, keepdims=True)
        * (float(rows) ** -0.5)
        / gain_ref[:, own]
    )

    def sent(amount, semaphore):
        pltpu.make_async_copy(amount, amount, semaphore).wait()

    sent(xg.at[pl.ds(0, n_dp - 1)], xg_send)
    sent(statr.at[pl.ds(0, n_dp - 1)], st_send)

    @pl.when(s < last)
    def _():
        sent(x_ref, xp_send)
        sent(qbuf, q_send)

    @pl.when(s == last)
    def _():
        sent(qbuf.at[:, pl.ds(0, n_dp - 1)], q_send)

    @pl.when(s > 0)
    def _():
        sent(carry, back_send)
        sent(g1, g1_send)

    turned_out.wait()
    carry_out.wait()
    gout_out.wait()


def chain(n_sec, n_dp, cotangent, x, scales, gain, weight):
    rows, cols = x.shape
    width = n_dp * cols
    lanes = scales.shape[1]
    blocks = jnp.concatenate([cotangent, x], axis=0)
    factors = jnp.concatenate([gain, scales.reshape(1, rows)], axis=1)
    chunks, groups = rows // CHUNK, rows // GROUP
    vmem = pl.BlockSpec(memory_space=pltpu.VMEM)
    hbm = pl.BlockSpec(memory_space=pl.ANY)
    sem = pltpu.SemaphoreType.DMA
    return pl.pallas_call(
        functools.partial(chain_kernel, n_sec, n_dp, rows, cols),
        name="chain",
        out_shape=(
            jax.ShapeDtypeStruct((rows, cols), BF16),
            jax.ShapeDtypeStruct((rows, cols), BF16),
            jax.ShapeDtypeStruct((1, cols), F32),
            jax.ShapeDtypeStruct(scales.shape, F32),
            jax.ShapeDtypeStruct((width, rows), BF16),
        ),
        in_specs=[hbm] * 3,
        out_specs=(hbm, hbm, vmem, vmem, hbm),
        scratch_shapes=[
            pltpu.VMEM((rows, cols), BF16),
            pltpu.VMEM((1, rows), F32),
            pltpu.VMEM((1, width), F32),
            pltpu.VMEM((rows, cols), BF16),
            pltpu.VMEM((rows, cols), BF16),
            pltpu.VMEM((width, rows), BF16),
            pltpu.VMEM((width, cols), BF16),
            pltpu.VMEM((cols, width), BF16),
            pltpu.VMEM((n_dp, rows, cols), BF16),
            pltpu.VMEM((rows, width), BF16),
            pltpu.VMEM((rows, cols), F32),
            pltpu.VMEM((rows, cols), BF16),
            pltpu.VMEM((rows, lanes), F32),
            pltpu.VMEM((rows, lanes), F32),
            pltpu.VMEM((2 * chunks, n_dp + 1, CHUNK, cols), BF16),
            pltpu.VMEM((chunks, n_dp + 1, CHUNK, cols), BF16),
            pltpu.VMEM((8, cols), F32),
            pltpu.VMEM((8, cols), F32),
            pltpu.VMEM((8, lanes), F32),
            pltpu.VMEM((n_dp, 8, lanes), F32),
            sem((4,)), sem((n_dp,)), sem, sem((3, groups)), sem, sem, sem((2 * chunks,)), sem, sem, sem,
            sem, sem, sem, sem, sem((3,)),
        ],
        compiler_params=pltpu.CompilerParams(
            collective_id=0, has_side_effects=True, vmem_limit_bytes=VMEM_LIMIT
        ),
    )(blocks, factors, weight)


def weight_kernel(scale, normed, carry, grads, gain_grad, row_dot, w_out, g_out, gg_out, rd_out):
    w_out[...] = scale * jnp.dot(normed[...], carry[...], preferred_element_type=F32)

    @pl.when(pl.program_id(0) == 0)
    def _():
        g_out[...] = grads[...]
        gg_out[...] = gain_grad[...]
        rd_out[...] = row_dot[...]


def weight_grads(normed, carry, grads, gain_grad, row_dot):
    width, rows = normed.shape
    cols = carry.shape[1]
    part = width // WRITES
    whole = lambda a: pl.BlockSpec(a.shape, lambda k: (0, 0))
    return pl.pallas_call(
        functools.partial(weight_kernel, float(rows) ** -0.5),
        name="weight_grads",
        grid=(WRITES,),
        out_shape=(
            jax.ShapeDtypeStruct((width, cols), F32),
            jax.ShapeDtypeStruct(grads.shape, grads.dtype),
            jax.ShapeDtypeStruct(gain_grad.shape, F32),
            jax.ShapeDtypeStruct(row_dot.shape, F32),
        ),
        in_specs=[
            pl.BlockSpec((part, rows), lambda k: (k, 0)),
            whole(carry), whole(grads), whole(gain_grad), whole(row_dot),
        ],
        out_specs=(
            pl.BlockSpec((part, cols), lambda k: (k, 0)),
            whole(grads), whole(gain_grad), whole(row_dot),
        ),
        compiler_params=pltpu.CompilerParams(vmem_limit_bytes=VMEM_LIMIT),
    )(normed, carry, grads, gain_grad, row_dot)


def body(n_sec, n_dp, cotangent, inputs, inv_rms, gain, weight):
    micro, per, cols = cotangent.shape
    rows = micro * per
    carry, grads, gain_grad, row_dot, normed = chain(
        n_sec, n_dp, cotangent.reshape(rows, cols), inputs.reshape(rows, cols),
        inv_rms[0], gain, weight[0],
    )
    w_grad, grads, gain_grad, row_dot = weight_grads(normed, carry, grads, gain_grad, row_dot)
    return grads.reshape(1, micro, per, cols), w_grad[None], gain_grad, row_dot[None]


def solution(mesh):
    return jax.shard_map(
        functools.partial(body, mesh.shape["section"], mesh.shape["dp"]),
        mesh=mesh,
        in_specs=(
            P(None, None, "dp"),
            P("section", None, None, "dp"),
            P("section", None, None),
            P("section", None),
            P("section", None, "dp"),
        ),
        out_specs=(
            P("section", None, None, "dp"),
            P("section", None, "dp"),
            P("section", "dp"),
            P("section", None, None),
        ),
        check_vma=False,
    )
```
